32 devices in a mesh: seq: 16 (over z, y, x), tp: 2 (over core).
Axes of the slice: x: 2, y: 2, z: 4, core: 2. Of those that a mesh axis runs over, the one named last changes fastest.
Arguments:
- queries: bfloat16 [4096, 4096], P('seq', 'tp'), may hold values from -50 to 50
- keys: bfloat16 [4096, 4096], P('seq', 'tp'), may hold values from -4 to 4
- values: bfloat16 [4096, 4096], P('seq', 'tp'), may hold values from -18 to 18
- doc_lengths: int32 [32], replicated, may hold values from 1 to 2048, 4096 in all
- out_weight: bfloat16 [4096, 4096], P('tp', 'seq'), may hold values from -0.125 to 0.125
Outputs:
- projected: bfloat16 [4096, 4096], P('seq', 'tp')
The draws below stay inside these ranges and needn't reach their ends.
Inputs may be any that keep to these rules, and one draw needn't show every extreme that they name: `doc_lengths`: document lengths in order, summing to 4096; the longest is exactly 2048.
All inputs are finite; a program needn't handle non-finite values.
Results may differ from the reference program's by a relative error of at most 0.015.
Values may be sent and summed in bfloat16 or wider, within the bound.
A program may use at most 128 MiB of HBM per device.

```python
import math
import jax
import jax.numpy as jnp
import numpy as np
from jax import lax

D = 4096
HEADS = 32
HD = 128
TOK_DEV = 256
NDOC = 32
MOST = 2048
TOKENS = 4096
HW = 4096


def draw_pair(key):
    base = jax.random.fold_in(key, 17)
    key_one, key_two = jax.random.split(base, 2)
    shape = (TOKENS, HEADS * HD)
    keys_f = jnp.clip(jax.random.normal(key_one, shape, jnp.float32), -4.0, 4.0)
    queries_f = jnp.clip(jax.random.normal(key_two, shape, jnp.float32), -4.0, 4.0)
    return (queries_f.astype(jnp.bfloat16), keys_f.astype(jnp.bfloat16))


def draw_queries(key, part):
    return draw_pair(key)[0]


def draw_keys(key, part):
    return draw_pair(key)[1]


def spiked(values, rng, source, target, parts, factor):
    owner, partner = [(jnp.arange(values.shape[dim]) // (values.shape[dim] // parts)).reshape([-1 if axis == dim else 1 for axis in range(values.ndim)]) for dim in (source, target)]
    chosen = jax.random.permutation(rng, parts)[partner]
    strong = (owner == chosen) | (owner == (partner + parts // 2) % parts)
    return jnp.where(strong, factor * values, values)


def shard_levels(own_key, shape, cuts, least, high):
    def one(dim, blocks):
        steps = jax.random.uniform(jax.random.fold_in(jax.random.fold_in(own_key, 6), dim), (blocks,), jnp.float32, least / len(cuts), high / len(cuts))
        return jnp.repeat(jnp.exp(steps), shape[dim] // blocks).reshape((-1,) + (1,) * (len(shape) - dim - 1))

    gain = one(*cuts[0])
    for cut in cuts[1:]:
        gain = gain * one(*cut)
    return gain


def length_profile(number_of, total, limit, lean):
    weights = [(1 << 20) // math.isqrt(standing ** lean) + 1 for standing in range(2, number_of + 1)]
    spare, given = total - limit - (number_of - 1), [1] * (number_of - 1)
    while spare > 0:
        candidates = [i for i in range(number_of - 1) if given[i] < limit]
        pool, budget = sum([weights[i] for i in candidates]), spare
        for i in candidates:
            extra = min(limit - given[i], max(1, budget * weights[i] // pool), spare)
            given[i] = given[i] + extra
            spare = spare - extra
    return np.array([limit] + given)


def ragged(stream_key, count, total, reach, skew):
    if count == 2:
        one = jax.random.randint(stream_key, (), max(1, total - reach), min(reach, total - 1) + 1)
        return jnp.stack([one, total - one])
    lengths = jnp.asarray(length_profile(count, total, reach, skew), jnp.int32)
    twos = (count - 1) // 2
    source_of, taker = lengths[1:1 + 2 * twos:2], lengths[2:2 + 2 * twos:2]
    margin = jnp.minimum(source_of - 1, reach - taker)
    moved = jax.random.randint(jax.random.fold_in(stream_key, 1), (twos,), 0, 1 << 20) % (margin + 1)
    lengths = lengths.at[1:1 + 2 * twos:2].set(source_of - moved).at[2:2 + 2 * twos:2].set(taker + moved)
    return lengths[jax.random.permutation(jax.random.fold_in(stream_key, 2), count)]


def noise(stream_key, dims, width, bound, cuts=(), held_as=jnp.bfloat16):
    drawn = jax.random.normal(stream_key, dims, jnp.float32) * width
    if len(cuts) > 0:
        drawn = shard_levels(stream_key, dims, cuts, -0.22, 0.18) * drawn
    return jnp.clip(drawn, min=-bound, max=bound).astype(held_as)


def bell_draw_with(stream_key, dims, deviation, most, cuts, heavy, kind=jnp.bfloat16):
    drawn = deviation * jax.random.normal(stream_key, dims, jnp.float32)
    if cuts:
        drawn = drawn * shard_levels(stream_key, dims, cuts, -0.22, 0.18)
    return jnp.clip(spiked(drawn, jax.random.fold_in(stream_key, 3), *heavy), -most, most).astype(kind)


def setup_inputs(seed: int = 0) -> dict:
    key_of = jax.random.split(jax.random.key(seed), 6)
    queries = draw_queries(jax.random.fold_in(key_of[5], 71), 0)
    keys = draw_keys(jax.random.fold_in(key_of[5], 71), 0)
    values = noise(key_of[2], (TOKENS, HW), 3.0, 18.0, ((0, 16), (1, 2)))
    doc_lengths = ragged(key_of[3], NDOC, TOKENS, MOST, 2).astype(jnp.int32)
    out_weight = bell_draw_with(key_of[4], (HW, D), HW ** -0.5, 0.125, ((0, 2), (1, 16)), (0, 1, 16, 2.0))
    return dict(queries=queries, keys=keys, values=values, doc_lengths=doc_lengths, out_weight=out_weight)


def doc_of(positions, doc_lengths):
    ends = jnp.cumsum(doc_lengths).astype(jnp.int32)
    return jnp.sum((ends[None, :] <= positions[:, None]).astype(jnp.int32), axis=1).astype(jnp.int32)


def reference(queries, keys, values, doc_lengths, out_weight):
    scale = 1.0 / (HD ** 0.5)
    token_ids = doc_of(jnp.arange(TOKENS, dtype=jnp.int32), doc_lengths)
    pad_rows = jnp.zeros((MOST, HEADS * HD), jnp.bfloat16)
    keys_pad = jnp.concatenate([pad_rows, keys, pad_rows], axis=0)
    values_pad = jnp.concatenate([pad_rows, values, pad_rows], axis=0)
    pad_ids = jnp.full((MOST,), -1, jnp.int32)
    ids_pad = jnp.concatenate([pad_ids, token_ids, pad_ids], axis=0)
    span = TOK_DEV + 2 * MOST

    def one_block(block):
        start = (block * TOK_DEV).astype(jnp.int32)
        query_blk = lax.dynamic_slice_in_dim(queries, start, TOK_DEV, 0).astype(jnp.float32).reshape(TOK_DEV, HEADS, HD)
        key_blk = lax.dynamic_slice_in_dim(keys_pad, start, span, 0).astype(jnp.float32).reshape(span, HEADS, HD)
        value_blk = lax.dynamic_slice_in_dim(values_pad, start, span, 0).astype(jnp.float32).reshape(span, HEADS, HD)
        query_ids = lax.dynamic_slice_in_dim(token_ids, start, TOK_DEV, 0)
        key_ids = lax.dynamic_slice_in_dim(ids_pad, start, span, 0)
        same = (query_ids[:, None] == key_ids[None, :])[None]
        scores = jnp.einsum("qhd,khd->hqk", query_blk, key_blk) * scale
        scores = jnp.where(same, scores, -1e30)
        top = jnp.max(scores, axis=2, keepdims=True)
        weights = jnp.where(same, jnp.exp(scores - top), 0.0)
        totals = jnp.sum(weights, axis=2)
        rounded = lax.optimization_barrier(weights.astype(jnp.bfloat16)).astype(jnp.float32)
        mixed = jnp.einsum("hqk,khd->hqd", rounded, value_blk) / totals[:, :, None]
        return jnp.transpose(mixed, (1, 0, 2)).reshape(TOK_DEV, HEADS * HD).astype(jnp.bfloat16)

    attended = lax.map(one_block, jnp.arange(TOKENS // TOK_DEV, dtype=jnp.int32)).reshape(TOKENS, HEADS * HD)
    return jnp.dot(attended, out_weight, preferred_element_type=jnp.float32).astype(jnp.bfloat16)
```

```python
import functools
import math

import jax
import jax.numpy as jnp
from jax import lax
from jax.experimental import pallas as pl
from jax.experimental.pallas import tpu as pltpu
from jax.sharding import PartitionSpec as P

HD = 128
SCALE2 = math.log2(math.e) / math.sqrt(HD)


def ends_of(doc_lengths):
    count = doc_lengths.shape[0]
    before = jnp.arange(count)[None, :] <= jnp.arange(count)[:, None]
    return jnp.sum(jnp.where(before, doc_lengths[None, :], 0), axis=1)


def doc_of(positions, doc_lengths):
    ends = ends_of(doc_lengths)
    return jnp.sum((ends[None, :] <= positions[:, None]).astype(jnp.int32), axis=1)


def absorb(carry, query_heads, query_ids, key_heads, value_heads, key_ids):
    run_max, run_sum, accum = carry
    scale = 1.0 / math.sqrt(HD)
    scores = (
        jnp.einsum("qhd,khd->hqk", query_heads, key_heads, preferred_element_type=jnp.float32)
        * scale
    )
    same = (query_ids[:, None] == key_ids[None, :])[None]
    scores = jnp.where(same, scores, -1e30)
    new_max = jnp.maximum(run_max, jnp.max(scores, axis=2))
    weights = jnp.where(same, jnp.exp(scores - new_max[:, :, None]), 0.0)
    factor = jnp.exp(run_max - new_max)
    run_sum = run_sum * factor + jnp.sum(weights, axis=2)
    accum = accum * factor[:, :, None] + jnp.einsum(
        "hqk,khd->hqd",
        weights.astype(jnp.bfloat16),
        value_heads,
        preferred_element_type=jnp.float32,
    )
    return (new_max, run_sum, accum)


def attend_gathered(queries, keys, values, doc_lengths):
    rows = queries.shape[0]
    heads_here = queries.shape[1] // HD
    index = lax.axis_index("seq")
    query_heads = queries.reshape(rows, heads_here, HD)
    query_ids = doc_of(index * rows + jnp.arange(rows, dtype=jnp.int32), doc_lengths)

    def absorb_block(carry, key_rows, value_rows, key_ids):
        key_heads = key_rows.reshape(key_rows.shape[0], heads_here, HD)
        value_heads = value_rows.reshape(value_rows.shape[0], heads_here, HD)
        return absorb(carry, query_heads, query_ids, key_heads, value_heads, key_ids)

    start_state = (
        jnp.full((heads_here, rows), -1e30, jnp.float32),
        jnp.zeros((heads_here, rows), jnp.float32),
        jnp.zeros((heads_here, rows, HD), jnp.float32),
    )
    piece_keys = lax.all_gather(keys, "seq", axis=0, tiled=True)
    piece_values = lax.all_gather(values, "seq", axis=0, tiled=True)
    piece_rows = piece_keys.shape[0]
    span = 2 * rows

    def step_block(number, state):
        offset = number * span
        block_keys = lax.dynamic_slice_in_dim(piece_keys, offset, span, 0)
        block_values = lax.dynamic_slice_in_dim(piece_values, offset, span, 0)
        block_ids = doc_of(offset + jnp.arange(span, dtype=jnp.int32), doc_lengths)
        return absorb_block(state, block_keys, block_values, block_ids)

    run_max, run_sum, accum = lax.fori_loop(0, piece_rows // span, step_block, start_state)
    mixed = accum / run_sum[:, :, None]
    return jnp.transpose(mixed, (1, 0, 2)).reshape(rows, heads_here * HD).astype(jnp.bfloat16)


def attend_kernel(bk, low_ref, high_ref, q_ref, k_ref, v_ref, qid_ref, kid_ref, o_ref):
    bq = q_ref.shape[0]
    i = pl.program_id(1)
    own = (i * bq) // bk
    q = q_ref[...]
    qid = qid_ref[...]

    def part(j):
        start = pl.multiple_of(j * bk, bk)
        s = lax.dot_general(
            q, k_ref[pl.ds(start, bk), :], (((1,), (1,)), ((), ())),
            preferred_element_type=jnp.float32,
        )
        kid = kid_ref[j]
        s = jnp.where(qid == kid, s, -1e30)
        return s, v_ref[pl.ds(start, bk), :]

    s, v = part(own)
    m = jnp.max(s, axis=1, keepdims=True)
    p = jnp.exp2((s - m) * SCALE2)
    total = jnp.sum(p, axis=1, keepdims=True)
    acc = jnp.dot(p.astype(jnp.bfloat16), v, preferred_element_type=jnp.float32)

    def step(n, state):
        m, total, acc = state
        j = jnp.where(n >= own, n + 1, n)
        s, v = part(j)
        new = jnp.maximum(m, jnp.max(s, axis=1, keepdims=True))
        p = jnp.exp2((s - new) * SCALE2)
        factor = jnp.exp2((m - new) * SCALE2)
        total = total * factor + jnp.sum(p, axis=1, keepdims=True)
        acc = acc * factor + jnp.dot(
            p.astype(jnp.bfloat16), v, preferred_element_type=jnp.float32
        )
        return new, total, acc

    m, total, acc = lax.fori_loop(low_ref[i], high_ref[i], step, (m, total, acc))
    o_ref[...] = (acc / total).astype(o_ref.dtype)


def attend_heads(q, k, v, doc_lengths):
    tokens, width = q.shape
    bq = math.gcd(tokens, 256)
    bk = math.gcd(tokens, 512)
    ids = doc_of(jnp.arange(tokens, dtype=jnp.int32), doc_lengths)
    ends = ends_of(doc_lengths)
    starts = ends - doc_lengths
    firsts = jnp.arange(tokens // bq, dtype=jnp.int32) * bq
    lasts = firsts + bq - 1
    low = jnp.max(jnp.where(starts[None, :] <= firsts[:, None], starts[None, :], 0), axis=1) // bk
    high = (jnp.min(jnp.where(ends[None, :] > lasts[:, None], ends[None, :], tokens), axis=1) - 1) // bk
    grid_spec = pltpu.PrefetchScalarGridSpec(
        num_scalar_prefetch=2,
        grid=(width // HD, tokens // bq),
        in_specs=[
            pl.BlockSpec((bq, HD), lambda h, i, *_: (i, h)),
            pl.BlockSpec((tokens, HD), lambda h, i, *_: (0, h)),
            pl.BlockSpec((tokens, HD), lambda h, i, *_: (0, h)),
            pl.BlockSpec((bq, 1), lambda h, i, *_: (i, 0)),
            pl.BlockSpec((tokens // bk, 1, bk), lambda h, i, *_: (0, 0, 0)),
        ],
        out_specs=pl.BlockSpec((bq, HD), lambda h, i, *_: (i, h)),
    )
    return pl.pallas_call(
        functools.partial(attend_kernel, bk),
        out_shape=jax.ShapeDtypeStruct((tokens, width), jnp.bfloat16),
        grid_spec=grid_spec,
        compiler_params=pltpu.CompilerParams(vmem_limit_bytes=32 << 20),
        cost_estimate=pl.CostEstimate(
            flops=tokens * tokens * width * 2, bytes_accessed=tokens * width * 8,
            transcendentals=tokens * tokens * width // HD // 2,
        ),
    )(low, high, q, k, v, ids[:, None], ids.reshape(tokens // bk, 1, bk))


def local(parts, queries, keys, values, doc_lengths, out_weight):
    heads_here = queries.shape[1] // HD
    weight = lax.all_gather(out_weight, "seq", axis=1, tiled=True)
    if heads_here % parts == 0:
        q, k, v = [
            lax.all_to_all(a, "seq", split_axis=1, concat_axis=0, tiled=True)
            for a in (queries, keys, values)
        ]
        mixed = attend_heads(q, k, v, doc_lengths)
        attended = lax.all_to_all(mixed, "seq", split_axis=0, concat_axis=1, tiled=True)
    else:
        attended = attend_gathered(queries, keys, values, doc_lengths)
    partial_value = jnp.dot(attended, weight, preferred_element_type=jnp.float32)
    return lax.psum_scatter(
        partial_value.astype(jnp.bfloat16), "tp", scatter_dimension=1, tiled=True
    )


def solution(mesh):
    in_specs = (P("seq", "tp"), P("seq", "tp"), P("seq", "tp"), P(), P("tp", "seq"))
    out_specs = P("seq", "tp")
    return jax.shard_map(
        functools.partial(local, mesh.shape["seq"]),
        mesh=mesh, in_specs=in_specs, out_specs=out_specs, check_vma=False,
    )
```

```python
import functools
import math

import jax
import jax.numpy as jnp
from jax import lax
from jax.experimental import pallas as pl
from jax.experimental.pallas import tpu as pltpu
from jax.sharding import PartitionSpec as P

HD = 128
MESH = pl.DeviceIdType.MESH
SCALE2 = math.log2(math.e) / math.sqrt(HD)


def ends_of(doc_lengths):
    count = doc_lengths.shape[0]
    before = jnp.arange(count)[None, :] <= jnp.arange(count)[:, None]
    return jnp.sum(jnp.where(before, doc_lengths[None, :], 0), axis=1)


def doc_of(positions, doc_lengths):
    ends = ends_of(doc_lengths)
    return jnp.sum((ends[None, :] <= positions[:, None]).astype(jnp.int32), axis=1)


def absorb(carry, query_heads, query_ids, key_heads, value_heads, key_ids):
    run_max, run_sum, accum = carry
    scale = 1.0 / math.sqrt(HD)
    scores = (
        jnp.einsum("qhd,khd->hqk", query_heads, key_heads, preferred_element_type=jnp.float32)
        * scale
    )
    same = (query_ids[:, None] == key_ids[None, :])[None]
    scores = jnp.where(same, scores, -1e30)
    new_max = jnp.maximum(run_max, jnp.max(scores, axis=2))
    weights = jnp.where(same, jnp.exp(scores - new_max[:, :, None]), 0.0)
    factor = jnp.exp(run_max - new_max)
    run_sum = run_sum * factor + jnp.sum(weights, axis=2)
    accum = accum * factor[:, :, None] + jnp.einsum(
        "hqk,khd->hqd",
        weights.astype(jnp.bfloat16),
        value_heads,
        preferred_element_type=jnp.float32,
    )
    return (new_max, run_sum, accum)


def attend_gathered(queries, keys, values, doc_lengths):
    rows = queries.shape[0]
    heads_here = queries.shape[1] // HD
    index = lax.axis_index("seq")
    query_heads = queries.reshape(rows, heads_here, HD)
    query_ids = doc_of(index * rows + jnp.arange(rows, dtype=jnp.int32), doc_lengths)

    def absorb_block(carry, key_rows, value_rows, key_ids):
        key_heads = key_rows.reshape(key_rows.shape[0], heads_here, HD)
        value_heads = value_rows.reshape(value_rows.shape[0], heads_here, HD)
        return absorb(carry, query_heads, query_ids, key_heads, value_heads, key_ids)

    start_state = (
        jnp.full((heads_here, rows), -1e30, jnp.float32),
        jnp.zeros((heads_here, rows), jnp.float32),
        jnp.zeros((heads_here, rows, HD), jnp.float32),
    )
    piece_keys = lax.all_gather(keys, "seq", axis=0, tiled=True)
    piece_values = lax.all_gather(values, "seq", axis=0, tiled=True)
    piece_rows = piece_keys.shape[0]
    span = 2 * rows

    def step_block(number, state):
        offset = number * span
        block_keys = lax.dynamic_slice_in_dim(piece_keys, offset, span, 0)
        block_values = lax.dynamic_slice_in_dim(piece_values, offset, span, 0)
        block_ids = doc_of(offset + jnp.arange(span, dtype=jnp.int32), doc_lengths)
        return absorb_block(state, block_keys, block_values, block_ids)

    run_max, run_sum, accum = lax.fori_loop(0, piece_rows // span, step_block, start_state)
    mixed = accum / run_sum[:, :, None]
    return jnp.transpose(mixed, (1, 0, 2)).reshape(rows, heads_here * HD).astype(jnp.bfloat16)


def attend_kernel(bk, low_ref, high_ref, q_ref, k_ref, v_ref, qid_ref, kid_ref, o_ref):
    bq = q_ref.shape[0]
    i = pl.program_id(1)
    own = (i * bq) // bk
    q = q_ref[...]
    qid = qid_ref[...]

    def part(j):
        start = pl.multiple_of(j * bk, bk)
        s = lax.dot_general(
            q, k_ref[pl.ds(start, bk), :], (((1,), (1,)), ((), ())),
            preferred_element_type=jnp.float32,
        )
        kid = kid_ref[j]
        s = jnp.where(qid == kid, s, -1e30)
        return s, v_ref[pl.ds(start, bk), :]

    s, v = part(own)
    m = jnp.max(s, axis=1, keepdims=True)
    p = jnp.exp2((s - m) * SCALE2)
    total = jnp.sum(p, axis=1, keepdims=True)
    acc = jnp.dot(p.astype(jnp.bfloat16), v, preferred_element_type=jnp.float32)

    def step(n, state):
        m, total, acc = state
        j = jnp.where(n >= own, n + 1, n)
        s, v = part(j)
        new = jnp.maximum(m, jnp.max(s, axis=1, keepdims=True))
        p = jnp.exp2((s - new) * SCALE2)
        factor = jnp.exp2((m - new) * SCALE2)
        total = total * factor + jnp.sum(p, axis=1, keepdims=True)
        acc = acc * factor + jnp.dot(
            p.astype(jnp.bfloat16), v, preferred_element_type=jnp.float32
        )
        return new, total, acc

    m, total, acc = lax.fori_loop(low_ref[i], high_ref[i], step, (m, total, acc))
    o_ref[...] = (acc / total).astype(o_ref.dtype)


def attend_heads(q, k, v, doc_lengths):
    tokens, width = q.shape
    bq = math.gcd(tokens, 256)
    bk = math.gcd(tokens, 512)
    ids = doc_of(jnp.arange(tokens, dtype=jnp.int32), doc_lengths)
    ends = ends_of(doc_lengths)
    starts = ends - doc_lengths
    firsts = jnp.arange(tokens // bq, dtype=jnp.int32) * bq
    lasts = firsts + bq - 1
    low = jnp.max(jnp.where(starts[None, :] <= firsts[:, None], starts[None, :], 0), axis=1) // bk
    high = (jnp.min(jnp.where(ends[None, :] > lasts[:, None], ends[None, :], tokens), axis=1) - 1) // bk
    grid_spec = pltpu.PrefetchScalarGridSpec(
        num_scalar_prefetch=2,
        grid=(width // HD, tokens // bq),
        in_specs=[
            pl.BlockSpec((bq, HD), lambda h, i, *_: (i, h)),
            pl.BlockSpec((tokens, HD), lambda h, i, *_: (0, h)),
            pl.BlockSpec((tokens, HD), lambda h, i, *_: (0, h)),
            pl.BlockSpec((bq, 1), lambda h, i, *_: (i, 0)),
            pl.BlockSpec((tokens // bk, 1, bk), lambda h, i, *_: (0, 0, 0)),
        ],
        out_specs=pl.BlockSpec((bq, HD), lambda h, i, *_: (i, h)),
    )
    return pl.pallas_call(
        functools.partial(attend_kernel, bk),
        out_shape=jax.ShapeDtypeStruct((tokens, width), jnp.bfloat16),
        grid_spec=grid_spec,
        compiler_params=pltpu.CompilerParams(vmem_limit_bytes=32 << 20),
        cost_estimate=pl.CostEstimate(
            flops=tokens * tokens * width * 2, bytes_accessed=tokens * width * 8,
            transcendentals=tokens * tokens * width // HD // 2,
        ),
    )(low, high, q, k, v, ids[:, None], ids.reshape(tokens // bk, 1, bk))


def greet(parts, me, tp_too):
    barrier = pltpu.get_barrier_semaphore()

    @pl.loop(1, parts)
    def _(step):
        pl.semaphore_signal(
            barrier, inc=1, device_id={"seq": lax.rem(me + step, parts)}, device_id_type=MESH
        )

    if tp_too:
        other = 1 - lax.axis_index("tp")
        pl.semaphore_signal(barrier, inc=1, device_id={"tp": other}, device_id_type=MESH)
    pl.semaphore_wait(barrier, parts - 1 + int(tp_too))


def spread_kernel(parts, q, k, v, q_out, k_out, v_out, send_sem, recv_sem, own_sem):
    me = lax.axis_index("seq")
    rows = q.shape[0]
    width = q_out.shape[1]
    pairs = ((q, q_out), (k, k_out), (v, v_out))

    def columns(p):
        return pl.ds(pl.multiple_of(p * width, width), width)

    def place(p):
        return pl.ds(pl.multiple_of(p * rows, rows), rows)

    greet(parts, me, False)

    @pl.loop(1, parts)
    def _(step):
        peer = lax.rem(me + step, parts)
        for n, (src, dst) in enumerate(pairs):
            pltpu.make_async_remote_copy(
                src_ref=src.at[:, columns(peer)], dst_ref=dst.at[place(me), :],
                send_sem=send_sem.at[n, peer], recv_sem=recv_sem.at[n, me],
                device_id={"seq": peer}, device_id_type=MESH,
            ).start()

    owns = [
        pltpu.make_async_copy(src.at[:, columns(me)], dst.at[place(me), :], own_sem.at[n])
        for n, (src, dst) in enumerate(pairs)
    ]
    for own in owns:
        own.start()
    for own in owns:
        own.wait()

    @pl.loop(1, parts)
    def _(step):
        peer = lax.rem(me + step, parts)
        source = lax.rem(me + parts - step, parts)
        for n, (src, dst) in enumerate(pairs):
            pltpu.make_async_remote_copy(
                src_ref=src.at[:, columns(peer)], dst_ref=dst.at[place(source), :],
                send_sem=send_sem.at[n, peer], recv_sem=recv_sem.at[n, source],
                device_id={"seq": peer}, device_id_type=MESH,
            ).wait()


def spread(parts, q, k, v):
    rows, features = q.shape
    shape = jax.ShapeDtypeStruct((rows * parts, features // parts), q.dtype)
    return pl.pallas_call(
        functools.partial(spread_kernel, parts),
        out_shape=[shape] * 3,
        in_specs=[pl.BlockSpec(memory_space=pl.ANY)] * 3,
        out_specs=[pl.BlockSpec(memory_space=pl.ANY)] * 3,
        scratch_shapes=[
            pltpu.SemaphoreType.DMA((3, parts)),
            pltpu.SemaphoreType.DMA((3, parts)),
            pltpu.SemaphoreType.DMA((3,)),
        ],
        compiler_params=pltpu.CompilerParams(collective_id=0, has_side_effects=True),
        cost_estimate=pl.CostEstimate(flops=0, bytes_accessed=q.size * 200, transcendentals=0),
    )(q, k, v)


def back_kernel(parts, group, mixed, out, send_sem, recv_sem, pass_sem, got_sem, own_sem):
    me = lax.axis_index("seq")
    width = mixed.shape[1]
    rows = mixed.shape[0] // parts
    mine = lax.rem(me, group)
    base = me - mine

    def block(member, source):
        return out.at[
            pl.ds(pl.multiple_of(member * rows, rows), rows),
            pl.ds(pl.multiple_of(source * width, width), width),
        ]

    def send(peer, source):
        return pltpu.make_async_remote_copy(
            src_ref=mixed.at[pl.ds(pl.multiple_of(peer * rows, rows), rows), :],
            dst_ref=block(lax.rem(peer, group), me),
            send_sem=send_sem.at[peer], recv_sem=recv_sem.at[me],
            device_id={"seq": peer}, device_id_type=MESH,
        )

    def hand_on(far, source):
        member = lax.rem(mine + far, group)
        return pltpu.make_async_remote_copy(
            src_ref=block(mine, source), dst_ref=block(mine, source),
            send_sem=pass_sem.at[member, source], recv_sem=got_sem.at[mine, source],
            device_id={"seq": base + member}, device_id_type=MESH,
        )

    greet(parts, me, False)

    @pl.loop(1, parts)
    def _(step):
        send(lax.rem(me + step, parts), me).start()

    own = pltpu.make_async_copy(
        mixed.at[pl.ds(pl.multiple_of(me * rows, rows), rows), :], block(mine, me), own_sem
    )
    own.start()
    own.wait()
    for far in range(1, group):
        hand_on(far, me).start()

    @pl.loop(1, parts)
    def _(step):
        source = lax.rem(me + parts - step, parts)
        pltpu.make_async_remote_copy(
            src_ref=block(mine, source), dst_ref=block(mine, source),
            send_sem=send_sem.at[source], recv_sem=recv_sem.at[source],
            device_id={"seq": source}, device_id_type=MESH,
        ).wait_recv()
        for far in range(1, group):
            hand_on(far, source).start()

    @pl.loop(1, parts)
    def _(step):
        send(lax.rem(me + step, parts), me).wait_send()

    @pl.loop(0, parts)
    def _(source):
        for far in range(1, group):
            hand_on(far, source).wait_send()
            member = lax.rem(mine + far, group)
            pltpu.make_async_remote_copy(
                src_ref=block(member, source), dst_ref=block(member, source),
                send_sem=pass_sem.at[member, source], recv_sem=got_sem.at[member, source],
                device_id={"seq": base + member}, device_id_type=MESH,
            ).wait_recv()


def back(parts, group, mixed):
    tokens, width = mixed.shape
    return pl.pallas_call(
        functools.partial(back_kernel, parts, group),
        out_shape=jax.ShapeDtypeStruct((tokens // parts * group, width * parts), mixed.dtype),
        in_specs=[pl.BlockSpec(memory_space=pl.ANY)],
        out_specs=pl.BlockSpec(memory_space=pl.ANY),
        scratch_shapes=[
            pltpu.SemaphoreType.DMA((parts,)),
            pltpu.SemaphoreType.DMA((parts,)),
            pltpu.SemaphoreType.DMA((group, parts)),
            pltpu.SemaphoreType.DMA((group, parts)),
            pltpu.SemaphoreType.DMA,
        ],
        compiler_params=pltpu.CompilerParams(collective_id=1, has_side_effects=True),
        cost_estimate=pl.CostEstimate(flops=0, bytes_accessed=mixed.size * 200, transcendentals=0),
    )(mixed)


def home_kernel(parts, group, part, out, came, summed, tp_send, tp_recv, send_sem, recv_sem):
    me = lax.axis_index("seq")
    half = lax.axis_index("tp")
    mine = lax.rem(me, group)
    base = me - mine
    rows, features = out.shape
    span = came.shape[2]
    piece = features // parts * 2
    runs = span // piece

    def keep(which):
        return pl.ds(pl.multiple_of(which * span, span), span)

    def swap(member):
        return pltpu.make_async_remote_copy(
            src_ref=part.at[pl.ds(pl.multiple_of(member * rows, rows), rows), keep(1 - half)],
            dst_ref=came.at[member],
            send_sem=tp_send.at[member], recv_sem=tp_recv.at[member],
            device_id={"tp": 1 - half}, device_id_type=MESH,
        )

    def target(member, run):
        at = (run * group + member) * piece
        return out.at[:, pl.ds(pl.multiple_of(at, piece), piece)]

    def send(member, run, to, sem):
        return pltpu.make_async_remote_copy(
            src_ref=summed.at[member, :, pl.ds(run * piece, piece)], dst_ref=target(sem, run),
            send_sem=send_sem.at[member, run], recv_sem=recv_sem.at[sem, run],
            device_id={"seq": to}, device_id_type=MESH,
        )

    greet(parts, me, True)
    order = [lax.rem(mine + far, group) for far in (*range(1, group), 0)]
    for member in order:
        swap(member).start()
    for member in order:
        swap(member).wait_recv()
        own = part[pl.ds(pl.multiple_of(member * rows, rows), rows), keep(half)]
        total = own.astype(jnp.float32) + came[member].astype(jnp.float32)
        if member is order[-1]:
            for run in range(runs):
                at = pl.multiple_of((run * group + mine) * piece, piece)
                out[:, pl.ds(at, piece)] = total[:, run * piece:(run + 1) * piece].astype(out.dtype)
        else:
            summed[member] = total.astype(summed.dtype)
            for run in range(runs):
                send(member, run, base + member, mine).start()
    for member in order[:-1]:
        for run in range(runs):
            send(member, run, base + member, mine).wait_send()
            send(member, run, base + member, member).wait_recv()
    for member in order:
        swap(member).wait_send()


def home(parts, group, rows, part):
    tall, wide = part.shape
    span = wide // 2
    features = span * group
    return pl.pallas_call(
        functools.partial(home_kernel, parts, group),
        out_shape=jax.ShapeDtypeStruct((rows, features), part.dtype),
        in_specs=[pl.BlockSpec(memory_space=pltpu.VMEM)],
        out_specs=pl.BlockSpec(memory_space=pltpu.VMEM),
        scratch_shapes=[
            pltpu.VMEM((group, rows, span), part.dtype),
            pltpu.VMEM((group, rows, span), part.dtype),
            pltpu.SemaphoreType.DMA((group,)),
            pltpu.SemaphoreType.DMA((group,)),
            pltpu.SemaphoreType.DMA((group, parts // group // 2)),
            pltpu.SemaphoreType.DMA((group, parts // group // 2)),
        ],
        compiler_params=pltpu.CompilerParams(
            collective_id=2, has_side_effects=True, vmem_limit_bytes=24 << 20
        ),
    )(part)


def local(parts, pair, queries, keys, values, doc_lengths, out_weight):
    rows, width = queries.shape
    group = math.isqrt(parts)
    if pair == 2 and group * group == parts and group % 2 == 0 and width // HD % parts == 0:
        across = [[m + group * n for n in range(group)] for m in range(group)]
        weight = lax.all_gather(
            out_weight, "seq", axis=1, tiled=True, axis_index_groups=across
        )
        q, k, v = spread(parts, queries, keys, values)
        mixed = attend_heads(q, k, v, doc_lengths)
        attended = back(parts, group, mixed)
        part = jnp.dot(attended, weight, preferred_element_type=jnp.float32)
        return home(parts, group, rows, part.astype(jnp.bfloat16))
    weight = lax.all_gather(out_weight, "seq", axis=1, tiled=True)
    attended = attend_gathered(queries, keys, values, doc_lengths)
    partial_value = jnp.dot(attended, weight, preferred_element_type=jnp.float32)
    return lax.psum_scatter(
        partial_value.astype(jnp.bfloat16), "tp", scatter_dimension=1, tiled=True
    )


def solution(mesh):
    in_specs = (P("seq", "tp"), P("seq", "tp"), P("seq", "tp"), P(), P("tp", "seq"))
    out_specs = P("seq", "tp")
    return jax.shard_map(
        functools.partial(local, mesh.shape["seq"], mesh.shape["tp"]),
        mesh=mesh, in_specs=in_specs, out_specs=out_specs, check_vma=False,
    )
```

```python
import functools
import math

import jax
import jax.numpy as jnp
from jax import lax
from jax.experimental import pallas as pl
from jax.experimental.pallas import tpu as pltpu
from jax.sharding import PartitionSpec as P

HD = 128
MESH = pl.DeviceIdType.MESH
SCALE2 = math.log2(math.e) / math.sqrt(HD)


def ends_of(doc_lengths):
    count = doc_lengths.shape[0]
    before = jnp.arange(count)[None, :] <= jnp.arange(count)[:, None]
    return jnp.sum(jnp.where(before, doc_lengths[None, :], 0), axis=1)


def doc_of(positions, doc_lengths):
    ends = ends_of(doc_lengths)
    return jnp.sum((ends[None, :] <= positions[:, None]).astype(jnp.int32), axis=1)


def absorb(carry, query_heads, query_ids, key_heads, value_heads, key_ids):
    run_max, run_sum, accum = carry
    scale = 1.0 / math.sqrt(HD)
    scores = (
        jnp.einsum("qhd,khd->hqk", query_heads, key_heads, preferred_element_type=jnp.float32)
        * scale
    )
    same = (query_ids[:, None] == key_ids[None, :])[None]
    scores = jnp.where(same, scores, -1e30)
    new_max = jnp.maximum(run_max, jnp.max(scores, axis=2))
    weights = jnp.where(same, jnp.exp(scores - new_max[:, :, None]), 0.0)
    factor = jnp.exp(run_max - new_max)
    run_sum = run_sum * factor + jnp.sum(weights, axis=2)
    accum = accum * factor[:, :, None] + jnp.einsum(
        "hqk,khd->hqd",
        weights.astype(jnp.bfloat16),
        value_heads,
        preferred_element_type=jnp.float32,
    )
    return (new_max, run_sum, accum)


def attend_gathered(queries, keys, values, doc_lengths):
    rows = queries.shape[0]
    heads_here = queries.shape[1] // HD
    index = lax.axis_index("seq")
    query_heads = queries.reshape(rows, heads_here, HD)
    query_ids = doc_of(index * rows + jnp.arange(rows, dtype=jnp.int32), doc_lengths)

    def absorb_block(carry, key_rows, value_rows, key_ids):
        key_heads = key_rows.reshape(key_rows.shape[0], heads_here, HD)
        value_heads = value_rows.reshape(value_rows.shape[0], heads_here, HD)
        return absorb(carry, query_heads, query_ids, key_heads, value_heads, key_ids)

    start_state = (
        jnp.full((heads_here, rows), -1e30, jnp.float32),
        jnp.zeros((heads_here, rows), jnp.float32),
        jnp.zeros((heads_here, rows, HD), jnp.float32),
    )
    piece_keys = lax.all_gather(keys, "seq", axis=0, tiled=True)
    piece_values = lax.all_gather(values, "seq", axis=0, tiled=True)
    piece_rows = piece_keys.shape[0]
    span = 2 * rows

    def step_block(number, state):
        offset = number * span
        block_keys = lax.dynamic_slice_in_dim(piece_keys, offset, span, 0)
        block_values = lax.dynamic_slice_in_dim(piece_values, offset, span, 0)
        block_ids = doc_of(offset + jnp.arange(span, dtype=jnp.int32), doc_lengths)
        return absorb_block(state, block_keys, block_values, block_ids)

    run_max, run_sum, accum = lax.fori_loop(0, piece_rows // span, step_block, start_state)
    mixed = accum / run_sum[:, :, None]
    return jnp.transpose(mixed, (1, 0, 2)).reshape(rows, heads_here * HD).astype(jnp.bfloat16)


def attend_kernel(bk, low_ref, high_ref, q_ref, k_ref, v_ref, qid_ref, kid_ref, o_ref):
    bq = q_ref.shape[0]
    i = pl.program_id(1)
    own = (i * bq) // bk
    q = q_ref[...]
    qid = qid_ref[...]

    def part(j):
        start = pl.multiple_of(j * bk, bk)
        s = lax.dot_general(
            q, k_ref[pl.ds(start, bk), :], (((1,), (1,)), ((), ())),
            preferred_element_type=jnp.float32,
        )
        kid = kid_ref[j]
        s = jnp.where(qid == kid, s, -1e30)
        return s, v_ref[pl.ds(start, bk), :]

    s, v = part(own)
    m = jnp.max(s, axis=1, keepdims=True)
    p = jnp.exp2((s - m) * SCALE2)
    total = jnp.sum(p, axis=1, keepdims=True)
    acc = jnp.dot(p.astype(jnp.bfloat16), v, preferred_element_type=jnp.float32)

    def step(n, state):
        m, total, acc = state
        j = jnp.where(n >= own, n + 1, n)
        s, v = part(j)
        new = jnp.maximum(m, jnp.max(s, axis=1, keepdims=True))
        p = jnp.exp2((s - new) * SCALE2)
        factor = jnp.exp2((m - new) * SCALE2)
        total = total * factor + jnp.sum(p, axis=1, keepdims=True)
        acc = acc * factor + jnp.dot(
            p.astype(jnp.bfloat16), v, preferred_element_type=jnp.float32
        )
        return new, total, acc

    m, total, acc = lax.fori_loop(low_ref[i], high_ref[i], step, (m, total, acc))
    o_ref[...] = (acc / total).astype(o_ref.dtype)


def attend_heads(q, k, v, doc_lengths):
    tokens, width = q.shape
    bq = math.gcd(tokens, 256)
    bk = math.gcd(tokens, 512)
    ids = doc_of(jnp.arange(tokens, dtype=jnp.int32), doc_lengths)
    ends = ends_of(doc_lengths)
    starts = ends - doc_lengths
    firsts = jnp.arange(tokens // bq, dtype=jnp.int32) * bq
    lasts = firsts + bq - 1
    low = jnp.max(jnp.where(starts[None, :] <= firsts[:, None], starts[None, :], 0), axis=1) // bk
    high = (jnp.min(jnp.where(ends[None, :] > lasts[:, None], ends[None, :], tokens), axis=1) - 1) // bk
    grid_spec = pltpu.PrefetchScalarGridSpec(
        num_scalar_prefetch=2,
        grid=(width // HD, tokens // bq),
        in_specs=[
            pl.BlockSpec((bq, HD), lambda h, i, *_: (i, h)),
            pl.BlockSpec((tokens, HD), lambda h, i, *_: (0, h)),
            pl.BlockSpec((tokens, HD), lambda h, i, *_: (0, h)),
            pl.BlockSpec((bq, 1), lambda h, i, *_: (i, 0)),
            pl.BlockSpec((tokens // bk, 1, bk), lambda h, i, *_: (0, 0, 0)),
        ],
        out_specs=pl.BlockSpec((bq, HD), lambda h, i, *_: (i, h)),
    )
    return pl.pallas_call(
        functools.partial(attend_kernel, bk),
        out_shape=jax.ShapeDtypeStruct((tokens, width), jnp.bfloat16),
        grid_spec=grid_spec,
        compiler_params=pltpu.CompilerParams(vmem_limit_bytes=32 << 20),
        cost_estimate=pl.CostEstimate(
            flops=tokens * tokens * width * 2, bytes_accessed=tokens * width * 8,
            transcendentals=tokens * tokens * width // HD // 2,
        ),
    )(low, high, q, k, v, ids[:, None], ids.reshape(tokens // bk, 1, bk))


def greet(parts, me):
    barrier = pltpu.get_barrier_semaphore()

    @pl.loop(1, parts)
    def _(step):
        pl.semaphore_signal(
            barrier, inc=1, device_id={"seq": lax.rem(me + step, parts)}, device_id_type=MESH
        )

    pl.semaphore_wait(barrier, parts - 1)


def spread_kernel(parts, q, k, v, q_out, k_out, v_out, send_sem, recv_sem, own_sem):
    me = lax.axis_index("seq")
    rows = q.shape[0]
    width = q_out.shape[1]
    pairs = ((q, q_out), (k, k_out), (v, v_out))

    def columns(p):
        return pl.ds(pl.multiple_of(p * width, width), width)

    def place(p):
        return pl.ds(pl.multiple_of(p * rows, rows), rows)

    greet(parts, me)

    @pl.loop(1, parts)
    def _(step):
        peer = lax.rem(me + step, parts)
        for n, (src, dst) in enumerate(pairs):
            pltpu.make_async_remote_copy(
                src_ref=src.at[:, columns(peer)], dst_ref=dst.at[place(me), :],
                send_sem=send_sem.at[n, peer], recv_sem=recv_sem.at[n, me],
                device_id={"seq": peer}, device_id_type=MESH,
            ).start()

    owns = [
        pltpu.make_async_copy(src.at[:, columns(me)], dst.at[place(me), :], own_sem.at[n])
        for n, (src, dst) in enumerate(pairs)
    ]
    for own in owns:
        own.start()
    for own in owns:
        own.wait()

    @pl.loop(1, parts)
    def _(step):
        peer = lax.rem(me + step, parts)
        source = lax.rem(me + parts - step, parts)
        for n, (src, dst) in enumerate(pairs):
            pltpu.make_async_remote_copy(
                src_ref=src.at[:, columns(peer)], dst_ref=dst.at[place(source), :],
                send_sem=send_sem.at[n, peer], recv_sem=recv_sem.at[n, source],
                device_id={"seq": peer}, device_id_type=MESH,
            ).wait()


def spread(parts, q, k, v):
    rows, features = q.shape
    shape = jax.ShapeDtypeStruct((rows * parts, features // parts), q.dtype)
    return pl.pallas_call(
        functools.partial(spread_kernel, parts),
        out_shape=[shape] * 3,
        in_specs=[pl.BlockSpec(memory_space=pl.ANY)] * 3,
        out_specs=[pl.BlockSpec(memory_space=pl.ANY)] * 3,
        scratch_shapes=[
            pltpu.SemaphoreType.DMA((3, parts)),
            pltpu.SemaphoreType.DMA((3, parts)),
            pltpu.SemaphoreType.DMA((3,)),
        ],
        compiler_params=pltpu.CompilerParams(collective_id=0, has_side_effects=True),
        cost_estimate=pl.CostEstimate(flops=0, bytes_accessed=q.size * 200, transcendentals=0),
    )(q, k, v)


def back_kernel(parts, group, mixed, out, send_sem, recv_sem, pass_sem, got_sem, own_sem):
    me = lax.axis_index("seq")
    width = mixed.shape[1]
    rows = mixed.shape[0] // parts
    mine = lax.rem(me, group)
    base = me - mine

    def block(member, source):
        return out.at[
            pl.ds(pl.multiple_of(member * rows, rows), rows),
            pl.ds(pl.multiple_of(source * width, width), width),
        ]

    def send(peer, source):
        return pltpu.make_async_remote_copy(
            src_ref=mixed.at[pl.ds(pl.multiple_of(peer * rows, rows), rows), :],
            dst_ref=block(lax.rem(peer, group), me),
            send_sem=send_sem.at[peer], recv_sem=recv_sem.at[me],
            device_id={"seq": peer}, device_id_type=MESH,
        )

    def hand_on(far, source):
        member = lax.rem(mine + far, group)
        return pltpu.make_async_remote_copy(
            src_ref=block(mine, source), dst_ref=block(mine, source),
            send_sem=pass_sem.at[member, source], recv_sem=got_sem.at[mine, source],
            device_id={"seq": base + member}, device_id_type=MESH,
        )

    greet(parts, me)

    @pl.loop(1, parts)
    def _(step):
        send(lax.rem(me + step, parts), me).start()

    own = pltpu.make_async_copy(
        mixed.at[pl.ds(pl.multiple_of(me * rows, rows), rows), :], block(mine, me), own_sem
    )
    own.start()
    own.wait()
    for far in range(1, group):
        hand_on(far, me).start()

    @pl.loop(1, parts)
    def _(step):
        source = lax.rem(me + parts - step, parts)
        pltpu.make_async_remote_copy(
            src_ref=block(mine, source), dst_ref=block(mine, source),
            send_sem=send_sem.at[source], recv_sem=recv_sem.at[source],
            device_id={"seq": source}, device_id_type=MESH,
        ).wait_recv()
        for far in range(1, group):
            hand_on(far, source).start()

    @pl.loop(1, parts)
    def _(step):
        send(lax.rem(me + step, parts), me).wait_send()

    @pl.loop(0, parts)
    def _(source):
        for far in range(1, group):
            hand_on(far, source).wait_send()
            member = lax.rem(mine + far, group)
            pltpu.make_async_remote_copy(
                src_ref=block(member, source), dst_ref=block(member, source),
                send_sem=pass_sem.at[member, source], recv_sem=got_sem.at[member, source],
                device_id={"seq": base + member}, device_id_type=MESH,
            ).wait_recv()


def back(parts, group, mixed):
    tokens, width = mixed.shape
    return pl.pallas_call(
        functools.partial(back_kernel, parts, group),
        out_shape=jax.ShapeDtypeStruct((tokens // parts * group, width * parts), mixed.dtype),
        in_specs=[pl.BlockSpec(memory_space=pl.ANY)],
        out_specs=pl.BlockSpec(memory_space=pl.ANY),
        scratch_shapes=[
            pltpu.SemaphoreType.DMA((parts,)),
            pltpu.SemaphoreType.DMA((parts,)),
            pltpu.SemaphoreType.DMA((group, parts)),
            pltpu.SemaphoreType.DMA((group, parts)),
            pltpu.SemaphoreType.DMA,
        ],
        compiler_params=pltpu.CompilerParams(collective_id=1, has_side_effects=True),
        cost_estimate=pl.CostEstimate(flops=0, bytes_accessed=mixed.size * 200, transcendentals=0),
    )(mixed)


def home_kernel(parts, group, part, out, came, summed, tp_send, tp_recv, send_sem, recv_sem):
    me = lax.axis_index("seq")
    half = lax.axis_index("tp")
    mine = lax.rem(me, group)
    base = me - mine
    rows, features = out.shape
    span = came.shape[2]
    piece = features // parts * 2
    runs = span // piece

    def keep(which):
        return pl.ds(pl.multiple_of(which * span, span), span)

    def swap(member):
        return pltpu.make_async_remote_copy(
            src_ref=part.at[pl.ds(pl.multiple_of(member * rows, rows), rows), keep(1 - half)],
            dst_ref=came.at[member],
            send_sem=tp_send.at[member], recv_sem=tp_recv.at[member],
            device_id={"tp": 1 - half}, device_id_type=MESH,
        )

    def target(member, run):
        at = (run * group + member) * piece
        return out.at[:, pl.ds(pl.multiple_of(at, piece), piece)]

    def send(member, run, to, sem):
        return pltpu.make_async_remote_copy(
            src_ref=summed.at[member, :, pl.ds(run * piece, piece)], dst_ref=target(sem, run),
            send_sem=send_sem.at[member, run], recv_sem=recv_sem.at[sem, run],
            device_id={"seq": to}, device_id_type=MESH,
        )

    barrier = pltpu.get_barrier_semaphore()
    pl.semaphore_signal(barrier, inc=1, device_id={"tp": 1 - half}, device_id_type=MESH)
    for far in range(1, group):
        pl.semaphore_signal(
            barrier, inc=1, device_id={"seq": base + lax.rem(mine + far, group)},
            device_id_type=MESH,
        )
    pl.semaphore_wait(barrier, group)
    order = [lax.rem(mine + far, group) for far in (*range(1, group), 0)]
    for member in order:
        swap(member).start()
    for member in order:
        swap(member).wait_recv()
        own = part[pl.ds(pl.multiple_of(member * rows, rows), rows), keep(half)]
        total = own.astype(jnp.float32) + came[member].astype(jnp.float32)
        if member is order[-1]:
            for run in range(runs):
                at = pl.multiple_of((run * group + mine) * piece, piece)
                out[:, pl.ds(at, piece)] = total[:, run * piece:(run + 1) * piece].astype(out.dtype)
        else:
            summed[member] = total.astype(summed.dtype)
            for run in range(runs):
                send(member, run, base + member, mine).start()
    for member in order[:-1]:
        for run in range(runs):
            send(member, run, base + member, mine).wait_send()
            send(member, run, base + member, member).wait_recv()
    for member in order:
        swap(member).wait_send()


def home(parts, group, rows, part):
    tall, wide = part.shape
    span = wide // 2
    features = span * group
    return pl.pallas_call(
        functools.partial(home_kernel, parts, group),
        out_shape=jax.ShapeDtypeStruct((rows, features), part.dtype),
        in_specs=[pl.BlockSpec(memory_space=pltpu.VMEM)],
        out_specs=pl.BlockSpec(memory_space=pltpu.VMEM),
        scratch_shapes=[
            pltpu.VMEM((group, rows, span), part.dtype),
            pltpu.VMEM((group, rows, span), part.dtype),
            pltpu.SemaphoreType.DMA((group,)),
            pltpu.SemaphoreType.DMA((group,)),
            pltpu.SemaphoreType.DMA((group, parts // group // 2)),
            pltpu.SemaphoreType.DMA((group, parts // group // 2)),
        ],
        compiler_params=pltpu.CompilerParams(
            collective_id=2, has_side_effects=True, vmem_limit_bytes=24 << 20
        ),
    )(part)


def local(parts, pair, queries, keys, values, doc_lengths, out_weight):
    rows, width = queries.shape
    group = math.isqrt(parts)
    if pair == 2 and group * group == parts and group % 2 == 0 and width // HD % parts == 0:
        across = [[m + group * n for n in range(group)] for m in range(group)]
        q, k, v = spread(parts, queries, keys, values)
        q, out_weight = lax.optimization_barrier((q, out_weight))
        weight = lax.all_gather(
            out_weight, "seq", axis=1, tiled=True, axis_index_groups=across
        )
        mixed = attend_heads(q, k, v, doc_lengths)
        attended = back(parts, group, mixed)
        part = jnp.dot(attended, weight, preferred_element_type=jnp.float32)
        return home(parts, group, rows, part.astype(jnp.bfloat16))
    weight = lax.all_gather(out_weight, "seq", axis=1, tiled=True)
    attended = attend_gathered(queries, keys, values, doc_lengths)
    partial_value = jnp.dot(attended, weight, preferred_element_type=jnp.float32)
    return lax.psum_scatter(
        partial_value.astype(jnp.bfloat16), "tp", scatter_dimension=1, tiled=True
    )


def solution(mesh):
    in_specs = (P("seq", "tp"), P("seq", "tp"), P("seq", "tp"), P(), P("tp", "seq"))
    out_specs = P("seq", "tp")
    return jax.shard_map(
        functools.partial(local, mesh.shape["seq"], mesh.shape["tp"]),
        mesh=mesh, in_specs=in_specs, out_specs=out_specs, check_vma=False,
    )
```

```python
import functools
import math

import jax
import jax.numpy as jnp
from jax import lax
from jax.experimental import pallas as pl
from jax.experimental.pallas import tpu as pltpu
from jax.sharding import PartitionSpec as P

HD = 128
MESH = pl.DeviceIdType.MESH
SCALE2 = math.log2(math.e) / math.sqrt(HD)


def ends_of(doc_lengths):
    count = doc_lengths.shape[0]
    before = jnp.arange(count)[None, :] <= jnp.arange(count)[:, None]
    return jnp.sum(jnp.where(before, doc_lengths[None, :], 0), axis=1)


def doc_of(positions, doc_lengths):
    ends = ends_of(doc_lengths)
    return jnp.sum((ends[None, :] <= positions[:, None]).astype(jnp.int32), axis=1)


def absorb(carry, query_heads, query_ids, key_heads, value_heads, key_ids):
    run_max, run_sum, accum = carry
    scale = 1.0 / math.sqrt(HD)
    scores = (
        jnp.einsum("qhd,khd->hqk", query_heads, key_heads, preferred_element_type=jnp.float32)
        * scale
    )
    same = (query_ids[:, None] == key_ids[None, :])[None]
    scores = jnp.where(same, scores, -1e30)
    new_max = jnp.maximum(run_max, jnp.max(scores, axis=2))
    weights = jnp.where(same, jnp.exp(scores - new_max[:, :, None]), 0.0)
    factor = jnp.exp(run_max - new_max)
    run_sum = run_sum * factor + jnp.sum(weights, axis=2)
    accum = accum * factor[:, :, None] + jnp.einsum(
        "hqk,khd->hqd",
        weights.astype(jnp.bfloat16),
        value_heads,
        preferred_element_type=jnp.float32,
    )
    return (new_max, run_sum, accum)


def attend_gathered(queries, keys, values, doc_lengths):
    rows = queries.shape[0]
    heads_here = queries.shape[1] // HD
    index = lax.axis_index("seq")
    query_heads = queries.reshape(rows, heads_here, HD)
    query_ids = doc_of(index * rows + jnp.arange(rows, dtype=jnp.int32), doc_lengths)

    def absorb_block(carry, key_rows, value_rows, key_ids):
        key_heads = key_rows.reshape(key_rows.shape[0], heads_here, HD)
        value_heads = value_rows.reshape(value_rows.shape[0], heads_here, HD)
        return absorb(carry, query_heads, query_ids, key_heads, value_heads, key_ids)

    start_state = (
        jnp.full((heads_here, rows), -1e30, jnp.float32),
        jnp.zeros((heads_here, rows), jnp.float32),
        jnp.zeros((heads_here, rows, HD), jnp.float32),
    )
    piece_keys = lax.all_gather(keys, "seq", axis=0, tiled=True)
    piece_values = lax.all_gather(values, "seq", axis=0, tiled=True)
    piece_rows = piece_keys.shape[0]
    span = 2 * rows

    def step_block(number, state):
        offset = number * span
        block_keys = lax.dynamic_slice_in_dim(piece_keys, offset, span, 0)
        block_values = lax.dynamic_slice_in_dim(piece_values, offset, span, 0)
        block_ids = doc_of(offset + jnp.arange(span, dtype=jnp.int32), doc_lengths)
        return absorb_block(state, block_keys, block_values, block_ids)

    run_max, run_sum, accum = lax.fori_loop(0, piece_rows // span, step_block, start_state)
    mixed = accum / run_sum[:, :, None]
    return jnp.transpose(mixed, (1, 0, 2)).reshape(rows, heads_here * HD).astype(jnp.bfloat16)


def attend_kernel(bk, low_ref, high_ref, q_ref, k_ref, v_ref, qid_ref, kid_ref, o_ref):
    bq = q_ref.shape[0]
    i = pl.program_id(1)
    own = (i * bq) // bk
    q = q_ref[...]
    qid = qid_ref[...]

    def part(j):
        start = pl.multiple_of(j * bk, bk)
        s = lax.dot_general(
            q, k_ref[pl.ds(start, bk), :], (((1,), (1,)), ((), ())),
            preferred_element_type=jnp.float32,
        )
        kid = kid_ref[j]
        s = jnp.where(qid == kid, s, -1e30)
        return s, v_ref[pl.ds(start, bk), :]

    s, v = part(own)
    m = jnp.max(s, axis=1, keepdims=True)
    p = jnp.exp2((s - m) * SCALE2)
    total = jnp.sum(p, axis=1, keepdims=True)
    acc = jnp.dot(p.astype(jnp.bfloat16), v, preferred_element_type=jnp.float32)

    def step(n, state):
        m, total, acc = state
        j = jnp.where(n >= own, n + 1, n)
        s, v = part(j)
        new = jnp.maximum(m, jnp.max(s, axis=1, keepdims=True))
        p = jnp.exp2((s - new) * SCALE2)
        factor = jnp.exp2((m - new) * SCALE2)
        total = total * factor + jnp.sum(p, axis=1, keepdims=True)
        acc = acc * factor + jnp.dot(
            p.astype(jnp.bfloat16), v, preferred_element_type=jnp.float32
        )
        return new, total, acc

    m, total, acc = lax.fori_loop(low_ref[i], high_ref[i], step, (m, total, acc))
    o_ref[...] = (acc / total).astype(o_ref.dtype)


def attend_heads(q, k, v, doc_lengths):
    tokens, width = q.shape
    bq = math.gcd(tokens, 512)
    bk = math.gcd(tokens, 512)
    ids = doc_of(jnp.arange(tokens, dtype=jnp.int32), doc_lengths)
    ends = ends_of(doc_lengths)
    starts = ends - doc_lengths
    firsts = jnp.arange(tokens // bq, dtype=jnp.int32) * bq
    lasts = firsts + bq - 1
    low = jnp.max(jnp.where(starts[None, :] <= firsts[:, None], starts[None, :], 0), axis=1) // bk
    high = (jnp.min(jnp.where(ends[None, :] > lasts[:, None], ends[None, :], tokens), axis=1) - 1) // bk
    grid_spec = pltpu.PrefetchScalarGridSpec(
        num_scalar_prefetch=2,
        grid=(width // HD, tokens // bq),
        in_specs=[
            pl.BlockSpec((bq, HD), lambda h, i, *_: (i, h)),
            pl.BlockSpec((tokens, HD), lambda h, i, *_: (0, h)),
            pl.BlockSpec((tokens, HD), lambda h, i, *_: (0, h)),
            pl.BlockSpec((bq, 1), lambda h, i, *_: (i, 0)),
            pl.BlockSpec((tokens // bk, 1, bk), lambda h, i, *_: (0, 0, 0)),
        ],
        out_specs=pl.BlockSpec((bq, HD), lambda h, i, *_: (i, h)),
    )
    return pl.pallas_call(
        functools.partial(attend_kernel, bk),
        out_shape=jax.ShapeDtypeStruct((tokens, width), jnp.bfloat16),
        grid_spec=grid_spec,
        compiler_params=pltpu.CompilerParams(vmem_limit_bytes=32 << 20),
        cost_estimate=pl.CostEstimate(
            flops=tokens * tokens * width * 2, bytes_accessed=tokens * width * 8,
            transcendentals=tokens * tokens * width // HD // 2,
        ),
    )(low, high, q, k, v, ids[:, None], ids.reshape(tokens // bk, 1, bk))


def greet(parts, me):
    barrier = pltpu.get_barrier_semaphore()

    @pl.loop(1, parts)
    def _(step):
        pl.semaphore_signal(
            barrier, inc=1, device_id={"seq": lax.rem(me + step, parts)}, device_id_type=MESH
        )

    pl.semaphore_wait(barrier, parts - 1)


def spread_kernel(parts, q, k, v, q_out, k_out, v_out, send_sem, recv_sem, own_sem):
    me = lax.axis_index("seq")
    rows = q.shape[0]
    width = q_out.shape[1]
    pairs = ((q, q_out), (k, k_out), (v, v_out))

    def columns(p):
        return pl.ds(pl.multiple_of(p * width, width), width)

    def place(p):
        return pl.ds(pl.multiple_of(p * rows, rows), rows)

    greet(parts, me)

    @pl.loop(1, parts)
    def _(step):
        peer = lax.rem(me + step, parts)
        for n, (src, dst) in enumerate(pairs):
            pltpu.make_async_remote_copy(
                src_ref=src.at[:, columns(peer)], dst_ref=dst.at[place(me), :],
                send_sem=send_sem.at[n, peer], recv_sem=recv_sem.at[n, me],
                device_id={"seq": peer}, device_id_type=MESH,
            ).start()

    owns = [
        pltpu.make_async_copy(src.at[:, columns(me)], dst.at[place(me), :], own_sem.at[n])
        for n, (src, dst) in enumerate(pairs)
    ]
    for own in owns:
        own.start()
    for own in owns:
        own.wait()

    @pl.loop(1, parts)
    def _(step):
        peer = lax.rem(me + step, parts)
        source = lax.rem(me + parts - step, parts)
        for n, (src, dst) in enumerate(pairs):
            pltpu.make_async_remote_copy(
                src_ref=src.at[:, columns(peer)], dst_ref=dst.at[place(source), :],
                send_sem=send_sem.at[n, peer], recv_sem=recv_sem.at[n, source],
                device_id={"seq": peer}, device_id_type=MESH,
            ).wait()


def spread(parts, q, k, v):
    rows, features = q.shape
    shape = jax.ShapeDtypeStruct((rows * parts, features // parts), q.dtype)
    return pl.pallas_call(
        functools.partial(spread_kernel, parts),
        out_shape=[shape] * 3,
        in_specs=[pl.BlockSpec(memory_space=pl.ANY)] * 3,
        out_specs=[pl.BlockSpec(memory_space=pl.ANY)] * 3,
        scratch_shapes=[
            pltpu.SemaphoreType.DMA((3, parts)),
            pltpu.SemaphoreType.DMA((3, parts)),
            pltpu.SemaphoreType.DMA((3,)),
        ],
        compiler_params=pltpu.CompilerParams(collective_id=0, has_side_effects=True),
        cost_estimate=pl.CostEstimate(flops=0, bytes_accessed=q.size * 200, transcendentals=0),
    )(q, k, v)


def back_kernel(parts, group, mixed, out, send_sem, recv_sem, pass_sem, got_sem, own_sem):
    me = lax.axis_index("seq")
    width = mixed.shape[1]
    rows = mixed.shape[0] // parts
    mine = lax.rem(me, group)
    base = me - mine

    def block(member, source):
        return out.at[
            pl.ds(pl.multiple_of(member * rows, rows), rows),
            pl.ds(pl.multiple_of(source * width, width), width),
        ]

    def send(peer, source):
        return pltpu.make_async_remote_copy(
            src_ref=mixed.at[pl.ds(pl.multiple_of(peer * rows, rows), rows), :],
            dst_ref=block(lax.rem(peer, group), me),
            send_sem=send_sem.at[peer], recv_sem=recv_sem.at[me],
            device_id={"seq": peer}, device_id_type=MESH,
        )

    def hand_on(far, source):
        member = lax.rem(mine + far, group)
        return pltpu.make_async_remote_copy(
            src_ref=block(mine, source), dst_ref=block(mine, source),
            send_sem=pass_sem.at[member, source], recv_sem=got_sem.at[mine, source],
            device_id={"seq": base + member}, device_id_type=MESH,
        )

    greet(parts, me)

    @pl.loop(1, parts)
    def _(step):
        send(lax.rem(me + step, parts), me).start()

    own = pltpu.make_async_copy(
        mixed.at[pl.ds(pl.multiple_of(me * rows, rows), rows), :], block(mine, me), own_sem
    )
    own.start()
    own.wait()
    for far in range(1, group):
        hand_on(far, me).start()

    @pl.loop(1, parts)
    def _(step):
        source = lax.rem(me + parts - step, parts)
        pltpu.make_async_remote_copy(
            src_ref=block(mine, source), dst_ref=block(mine, source),
            send_sem=send_sem.at[source], recv_sem=recv_sem.at[source],
            device_id={"seq": source}, device_id_type=MESH,
        ).wait_recv()
        for far in range(1, group):
            hand_on(far, source).start()

    @pl.loop(1, parts)
    def _(step):
        send(lax.rem(me + step, parts), me).wait_send()

    @pl.loop(0, parts)
    def _(source):
        for far in range(1, group):
            hand_on(far, source).wait_send()
            member = lax.rem(mine + far, group)
            pltpu.make_async_remote_copy(
                src_ref=block(member, source), dst_ref=block(member, source),
                send_sem=pass_sem.at[member, source], recv_sem=got_sem.at[member, source],
                device_id={"seq": base + member}, device_id_type=MESH,
            ).wait_recv()


def back(parts, group, mixed):
    tokens, width = mixed.shape
    return pl.pallas_call(
        functools.partial(back_kernel, parts, group),
        out_shape=jax.ShapeDtypeStruct((tokens // parts * group, width * parts), mixed.dtype),
        in_specs=[pl.BlockSpec(memory_space=pl.ANY)],
        out_specs=pl.BlockSpec(memory_space=pl.ANY),
        scratch_shapes=[
            pltpu.SemaphoreType.DMA((parts,)),
            pltpu.SemaphoreType.DMA((parts,)),
            pltpu.SemaphoreType.DMA((group, parts)),
            pltpu.SemaphoreType.DMA((group, parts)),
            pltpu.SemaphoreType.DMA,
        ],
        compiler_params=pltpu.CompilerParams(collective_id=1, has_side_effects=True),
        cost_estimate=pl.CostEstimate(flops=0, bytes_accessed=mixed.size * 200, transcendentals=0),
    )(mixed)


def home_kernel(parts, group, part, out, came, summed, tp_send, tp_recv, send_sem, recv_sem):
    me = lax.axis_index("seq")
    half = lax.axis_index("tp")
    mine = lax.rem(me, group)
    base = me - mine
    rows, features = out.shape
    span = came.shape[2]
    piece = features // parts * 2
    runs = span // piece

    def keep(which):
        return pl.ds(pl.multiple_of(which * span, span), span)

    def swap(member):
        return pltpu.make_async_remote_copy(
            src_ref=part.at[pl.ds(pl.multiple_of(member * rows, rows), rows), keep(1 - half)],
            dst_ref=came.at[member],
            send_sem=tp_send.at[member], recv_sem=tp_recv.at[member],
            device_id={"tp": 1 - half}, device_id_type=MESH,
        )

    def target(member, run):
        at = (run * group + member) * piece
        return out.at[:, pl.ds(pl.multiple_of(at, piece), piece)]

    def send(member, run, to, sem):
        return pltpu.make_async_remote_copy(
            src_ref=summed.at[member, :, pl.ds(run * piece, piece)], dst_ref=target(sem, run),
            send_sem=send_sem.at[member, run], recv_sem=recv_sem.at[sem, run],
            device_id={"seq": to}, device_id_type=MESH,
        )

    barrier = pltpu.get_barrier_semaphore()
    pl.semaphore_signal(barrier, inc=1, device_id={"tp": 1 - half}, device_id_type=MESH)
    for far in range(1, group):
        pl.semaphore_signal(
            barrier, inc=1, device_id={"seq": base + lax.rem(mine + far, group)},
            device_id_type=MESH,
        )
    pl.semaphore_wait(barrier, group)
    order = [lax.rem(mine + far, group) for far in (*range(1, group), 0)]
    for member in order:
        swap(member).start()
    for member in order:
        swap(member).wait_recv()
        own = part[pl.ds(pl.multiple_of(member * rows, rows), rows), keep(half)]
        total = own.astype(jnp.float32) + came[member].astype(jnp.float32)
        if member is order[-1]:
            for run in range(runs):
                at = pl.multiple_of((run * group + mine) * piece, piece)
                out[:, pl.ds(at, piece)] = total[:, run * piece:(run + 1) * piece].astype(out.dtype)
        else:
            summed[member] = total.astype(summed.dtype)
            for run in range(runs):
                send(member, run, base + member, mine).start()
    for member in order[:-1]:
        for run in range(runs):
            send(member, run, base + member, mine).wait_send()
            send(member, run, base + member, member).wait_recv()
    for member in order:
        swap(member).wait_send()


def home(parts, group, rows, part):
    tall, wide = part.shape
    span = wide // 2
    features = span * group
    return pl.pallas_call(
        functools.partial(home_kernel, parts, group),
        out_shape=jax.ShapeDtypeStruct((rows, features), part.dtype),
        in_specs=[pl.BlockSpec(memory_space=pltpu.VMEM)],
        out_specs=pl.BlockSpec(memory_space=pltpu.VMEM),
        scratch_shapes=[
            pltpu.VMEM((group, rows, span), part.dtype),
            pltpu.VMEM((group, rows, span), part.dtype),
            pltpu.SemaphoreType.DMA((group,)),
            pltpu.SemaphoreType.DMA((group,)),
            pltpu.SemaphoreType.DMA((group, parts // group // 2)),
            pltpu.SemaphoreType.DMA((group, parts // group // 2)),
        ],
        compiler_params=pltpu.CompilerParams(
            collective_id=2, has_side_effects=True, vmem_limit_bytes=24 << 20
        ),
    )(part)


def local(parts, pair, queries, keys, values, doc_lengths, out_weight):
    rows, width = queries.shape
    group = math.isqrt(parts)
    if pair == 2 and group * group == parts and group % 2 == 0 and width // HD % parts == 0:
        across = [[m + group * n for n in range(group)] for m in range(group)]
        q, k, v = spread(parts, queries, keys, values)
        q, out_weight = lax.optimization_barrier((q, out_weight))
        weight = lax.all_gather(
            out_weight, "seq", axis=1, tiled=True, axis_index_groups=across
        )
        mixed = attend_heads(q, k, v, doc_lengths)
        attended = back(parts, group, mixed)
        part = jnp.dot(attended, weight, preferred_element_type=jnp.float32)
        return home(parts, group, rows, part.astype(jnp.bfloat16))
    weight = lax.all_gather(out_weight, "seq", axis=1, tiled=True)
    attended = attend_gathered(queries, keys, values, doc_lengths)
    partial_value = jnp.dot(attended, weight, preferred_element_type=jnp.float32)
    return lax.psum_scatter(
        partial_value.astype(jnp.bfloat16), "tp", scatter_dimension=1, tiled=True
    )


def solution(mesh):
    in_specs = (P("seq", "tp"), P("seq", "tp"), P("seq", "tp"), P(), P("tp", "seq"))
    out_specs = P("seq", "tp")
    return jax.shard_map(
        functools.partial(local, mesh.shape["seq"], mesh.shape["tp"]),
        mesh=mesh, in_specs=in_specs, out_specs=out_specs, check_vma=False,
    )
```
